32 devices in a mesh: rep: 8 (over z, x), tp: 4 (over y, core).
Axes of the slice: x: 2, y: 2, z: 4, core: 2. Of those that a mesh axis runs over, the one named last changes fastest.
Arguments:
- tokens: bfloat16 [4096, 2048], P(('rep', 'tp')), may hold values from -6 to 6
- cotangent: bfloat16 [4096, 2048], P(('rep', 'tp')), may hold values from -6 to 6
- gate_blocks: bfloat16 [448, 4, 128, 128], P(('rep', 'tp')), may hold values from -6 to 6
- up_blocks: bfloat16 [448, 4, 128, 128], P(('rep', 'tp')), may hold values from -6 to 6
- down_blocks: bfloat16 [448, 4, 128, 128], P(('rep', 'tp')), may hold values from -6 to 6
- gate_rows: int32 [56, 4], P('tp'), may hold values from 0 to 15, as said below
- up_rows: int32 [56, 4], P('tp'), may hold values from 0 to 15, as said below
- down_columns: int32 [56, 4], P('tp'), may hold values from 0 to 15, as said below
- step_index: int32 [1], replicated, may hold values from 0 to 999
Outputs:
- input_grad: bfloat16 [4096, 2048], P(('rep', 'tp'))
- new_gate: bfloat16 [448, 4, 128, 128], P(('rep', 'tp'))
- new_up: bfloat16 [448, 4, 128, 128], P(('rep', 'tp'))
- new_down: bfloat16 [448, 4, 128, 128], P(('rep', 'tp'))
The draws below stay inside these ranges and needn't reach their ends.
Inputs may be any that keep to these rules, and one draw needn't show every extreme that they name: `gate_rows`: each row lists 4 different block numbers; all rows together name every block number. `up_rows`: each row lists 4 different block numbers; all rows together name every block number. `down_columns`: each row lists 4 different block numbers; all rows together name every block number.
All inputs are finite; a program needn't handle non-finite values.
Results may differ from the reference program's by a relative error of at most 0.008.
Values may be sent and summed in bfloat16 or wider, within the bound.
A program may use at most 192 MiB of HBM per device.

```python
import jax
import jax.numpy as jnp
from jax import lax

D = 2048
BLK = 128
ROWS = 512
REPLICAS = 8
TOKENS = 4096
DB = 16
FFB = 56
KEEP = 4
WBLOCKS = 448


def block_choice(key):
    base_key, rows_key = jax.random.split(key)
    starts = jax.random.permutation(base_key, DB).astype(jnp.int32)
    row_keys = jax.random.split(rows_key, FFB)

    def one_row(row_key, position):
        order = jax.random.permutation(row_key, DB - 1).astype(jnp.int32) + 1
        offsets = jnp.concatenate([jnp.zeros((1,), jnp.int32), order[:KEEP - 1]])
        first = starts[position % DB]
        return ((first + offsets) % DB).astype(jnp.int32)
    return jax.vmap(one_row)(row_keys, jnp.arange(FFB, dtype=jnp.int32))


def draw_gate_rows(key, part):
    return block_choice(jax.random.fold_in(key, 11))


def draw_up_rows(key, part):
    return block_choice(jax.random.fold_in(key, 23))


def draw_down_columns(key, part):
    return block_choice(jax.random.fold_in(key, 37))


def shard_levels(key, dims, pieces, smallest, high):
    def one(dim, shards_of):
        draws = jax.random.uniform(jax.random.fold_in(jax.random.fold_in(key, 6), dim), (shards_of,), jnp.float32, smallest / len(pieces), high / len(pieces))
        return jnp.repeat(jnp.exp(draws), dims[dim] // shards_of).reshape((-1,) + (1,) * (len(dims) - dim - 1))

    level = one(*pieces[0])
    for cut in pieces[1:]:
        level = level * one(*cut)
    return level


def bell_draw(key, shape, spread, reach, pieces=(), held_as=jnp.bfloat16):
    array = spread * jax.random.normal(key, shape, jnp.float32)
    if pieces:
        array = array * shard_levels(key, shape, pieces, -0.22, 0.18)
    return jnp.clip(array, -reach, reach).astype(held_as)


def setup_inputs(seed: int = 0) -> dict:
    seeds = jax.random.split(jax.random.key(seed), 10)
    tokens = bell_draw(seeds[0], (TOKENS, D), 1.0, 6.0, ((0, 32),))
    cotangent = bell_draw(seeds[1], (TOKENS, D), 1.0, 6.0, ((0, 32),))
    gate_blocks = bell_draw(seeds[2], (WBLOCKS, KEEP, BLK, BLK), 1.0, 6.0, ((0, 32),))
    up_blocks = bell_draw(seeds[3], (WBLOCKS, KEEP, BLK, BLK), 1.0, 6.0, ((0, 32),))
    down_blocks = bell_draw(seeds[4], (WBLOCKS, KEEP, BLK, BLK), 1.0, 6.0, ((0, 32),))
    gate_rows = draw_gate_rows(jax.random.fold_in(seeds[9], 71), 0)
    up_rows = draw_up_rows(jax.random.fold_in(seeds[9], 71), 0)
    down_columns = draw_down_columns(jax.random.fold_in(seeds[9], 71), 0)
    step_index = jax.random.randint(seeds[8], (1,), 0, 1000).astype(jnp.int32)
    return dict(tokens=tokens, cotangent=cotangent, gate_blocks=gate_blocks, up_blocks=up_blocks, down_blocks=down_blocks, gate_rows=gate_rows, up_rows=up_rows, down_columns=down_columns, step_index=step_index)


learn_rate = 0.5


def block_onehot(indices, count):
    return (indices[:, :, None] == jnp.arange(count, dtype=jnp.int32)[None, None, :]).astype(jnp.float32)


def replica_step(tokens_rep, cotangent_rep, gate_rep, up_rep, down_rep, gate_rows, up_rows, down_columns):
    weight_scale = (KEEP * BLK) ** -0.5
    token_blocks = tokens_rep.reshape(ROWS, DB, BLK)
    cotangent_blocks = cotangent_rep.reshape(ROWS, DB, BLK)
    gate_input = jnp.take(token_blocks, gate_rows, axis=1).astype(jnp.float32)
    up_input = jnp.take(token_blocks, up_rows, axis=1).astype(jnp.float32)
    down_input = jnp.take(cotangent_blocks, down_columns, axis=1).astype(jnp.float32)
    gate_weight = gate_rep.astype(jnp.float32)
    up_weight = up_rep.astype(jnp.float32)
    down_weight = down_rep.astype(jnp.float32)
    gate = weight_scale * jnp.einsum("rjkc,jkcd->rjd", gate_input, gate_weight)
    up = weight_scale * jnp.einsum("rjkc,jkcd->rjd", up_input, up_weight)
    sigmoid_gate = jax.nn.sigmoid(gate)
    activated = gate * sigmoid_gate
    hidden = (activated * up).astype(jnp.bfloat16)
    hidden_grad = weight_scale * jnp.einsum("rjkd,jkcd->rjc", down_input, down_weight)
    down_grad = (weight_scale * jnp.einsum("rjc,rjkd->jkcd", hidden.astype(jnp.float32), down_input)).astype(jnp.bfloat16)
    gate_signal = (hidden_grad * up * sigmoid_gate * (1.0 + gate * (1.0 - sigmoid_gate))).astype(jnp.bfloat16)
    up_signal = (hidden_grad * activated).astype(jnp.bfloat16)
    gate_grad = (weight_scale * jnp.einsum("rjkc,rjd->jkcd", gate_input, gate_signal.astype(jnp.float32))).astype(jnp.bfloat16)
    up_grad = (weight_scale * jnp.einsum("rjkc,rjd->jkcd", up_input, up_signal.astype(jnp.float32))).astype(jnp.bfloat16)
    gate_back = jnp.einsum("rjd,jkcd->rjkc", gate_signal.astype(jnp.float32), gate_weight)
    up_back = jnp.einsum("rjd,jkcd->rjkc", up_signal.astype(jnp.float32), up_weight)
    total = jnp.einsum("rjkc,jkb->rbc", gate_back, block_onehot(gate_rows, DB), precision=lax.Precision.HIGHEST)
    total = total + jnp.einsum("rjkc,jkb->rbc", up_back, block_onehot(up_rows, DB), precision=lax.Precision.HIGHEST)
    input_grad = (weight_scale * total).reshape(ROWS, D).astype(jnp.bfloat16)
    return input_grad, gate_grad, up_grad, down_grad


def averaged(weights, grads, step_index):
    levels = REPLICAS.bit_length() - 1
    distance = jnp.left_shift(jnp.int32(1), (step_index[0] % levels).astype(jnp.int32))
    peers = ((jnp.arange(REPLICAS, dtype=jnp.int32) - distance) % REPLICAS).astype(jnp.int32)
    updated = (weights.astype(jnp.float32) - learn_rate * grads.astype(jnp.float32)).astype(jnp.bfloat16)
    updated = lax.optimization_barrier(updated).astype(jnp.float32)
    return ((updated + jnp.take(updated, peers, axis=0)) * 0.5).astype(jnp.bfloat16)


def reference(tokens, cotangent, gate_blocks, up_blocks, down_blocks, gate_rows, up_rows, down_columns, step_index):
    shape_rep = (REPLICAS, FFB, KEEP, BLK, BLK)
    gate_all = gate_blocks.reshape(shape_rep)
    up_all = up_blocks.reshape(shape_rep)
    down_all = down_blocks.reshape(shape_rep)

    def one_replica(items):
        return replica_step(items[0], items[1], items[2], items[3], items[4], gate_rows, up_rows, down_columns)

    input_grad, gate_grad, up_grad, down_grad = lax.map(
        one_replica,
        (tokens.reshape(REPLICAS, ROWS, D), cotangent.reshape(REPLICAS, ROWS, D), gate_all, up_all, down_all))
    new_gate = averaged(gate_all, gate_grad, step_index).reshape(WBLOCKS, KEEP, BLK, BLK)
    new_up = averaged(up_all, up_grad, step_index).reshape(WBLOCKS, KEEP, BLK, BLK)
    new_down = averaged(down_all, down_grad, step_index).reshape(WBLOCKS, KEEP, BLK, BLK)
    return input_grad.reshape(TOKENS, D), new_gate, new_up, new_down
```

```python
import functools

import jax
import jax.numpy as jnp
from jax import lax
from jax.experimental import pallas as pl
from jax.experimental.pallas import tpu as pltpu
from jax.sharding import PartitionSpec as P

LEARN_RATE = 0.5
PIECES = 4
FIRST = 2
LATER = 3
VMEM_LIMIT = 60 * 1024 * 1024
F32 = jnp.float32
BF16 = jnp.bfloat16


def gather_kernel(rows, tok, cot, all_tok, all_cot, own_sem, sib_send, sib_recv, far_send, far_recv, fwd_send, fwd_recv):
    me = lax.axis_index("tp")
    sibling = me + 1 - 2 * lax.rem(me, 2)
    far = lax.rem(me + 2, 4)
    barrier = pltpu.get_barrier_semaphore()
    for other in (sibling, far):
        pl.semaphore_signal(barrier, inc=1, device_id={"tp": other}, device_id_type=pl.DeviceIdType.MESH)
    pl.semaphore_wait(barrier, 2)
    pairs = ((tok, all_tok), (cot, all_cot))
    part = rows // PIECES
    far_copies = []
    for a, (own, gathered) in enumerate(pairs):
        for i in range(PIECES):
            span = pl.ds(i * part, part)
            copy = pltpu.make_async_remote_copy(
                src_ref=own.at[span],
                dst_ref=gathered.at[me, span],
                send_sem=far_send.at[a, i],
                recv_sem=far_recv.at[a, i],
                device_id={"tp": far},
                device_id_type=pl.DeviceIdType.MESH,
            )
            copy.start()
            far_copies.append(copy)
    near_copies = []
    own_copies = []
    for a, (own, gathered) in enumerate(pairs):
        copy = pltpu.make_async_remote_copy(
            src_ref=own,
            dst_ref=gathered.at[me],
            send_sem=sib_send.at[a],
            recv_sem=sib_recv.at[a],
            device_id={"tp": sibling},
            device_id_type=pl.DeviceIdType.MESH,
        )
        copy.start()
        near_copies.append(copy)
        mine = pltpu.make_async_copy(own, gathered.at[me], own_sem.at[a])
        mine.start()
        own_copies.append(mine)
    forwards = []
    for a, (own, gathered) in enumerate(pairs):
        for i in range(PIECES):
            far_copies[a * PIECES + i].wait_recv()
            span = pl.ds(i * part, part)
            copy = pltpu.make_async_remote_copy(
                src_ref=gathered.at[far, span],
                dst_ref=gathered.at[far, span],
                send_sem=fwd_send.at[a, i],
                recv_sem=fwd_recv.at[a, i],
                device_id={"tp": sibling},
                device_id_type=pl.DeviceIdType.MESH,
            )
            copy.start()
            forwards.append(copy)
    for copy in far_copies:
        copy.wait_send()
    for copy in near_copies + own_copies + forwards:
        copy.wait()


def gathered_rows(tokens, cotangent):
    rows, width = tokens.shape
    count = lax.axis_size("tp")
    assert count == 4
    shape = jax.ShapeDtypeStruct((count, rows, width), tokens.dtype)
    dma = pltpu.SemaphoreType.DMA
    both = pl.pallas_call(
        functools.partial(gather_kernel, rows),
        out_shape=(shape, shape),
        in_specs=[pl.BlockSpec(memory_space=pl.ANY)] * 2,
        out_specs=(pl.BlockSpec(memory_space=pl.ANY),) * 2,
        scratch_shapes=[
            dma((2,)),
            dma((2,)),
            dma((2,)),
            dma((2, PIECES)),
            dma((2, PIECES)),
            dma((2, PIECES)),
            dma((2, PIECES)),
        ],
        compiler_params=pltpu.CompilerParams(collective_id=0, has_side_effects=True),
    )(tokens, cotangent)
    return [part.reshape(count * rows, width) for part in both]


def dot(a, b, dims):
    return lax.dot_general(a, b, (dims, ((), ())), preferred_element_type=F32)


def step_kernel(offset, first, keep, edge, gate_rows, up_rows, down_columns, x, g, wg, wu, wd, *rest):
    fresh, total = rest[-2:]
    scale = (keep * edge) ** (-0.5)
    j = offset + pl.program_id(0)

    @pl.when(pl.program_id(0) == 0)
    def _():
        total[...] = jnp.zeros_like(total) if first else rest[0][...]

    def picked(source, rows):
        return jnp.concatenate(
            [source[:, pl.ds(pl.multiple_of(rows[j, k] * edge, edge), edge)] for k in range(keep)], axis=1
        )

    def flat(w):
        return w[0].reshape(keep * edge, edge)

    gate_in = picked(x, gate_rows)
    up_in = picked(x, up_rows)
    down_in = picked(g, down_columns)
    gate = scale * dot(gate_in, flat(wg), ((1,), (0,)))
    up = scale * dot(up_in, flat(wu), ((1,), (0,)))
    hidden_grad = jnp.zeros_like(gate)
    for k in range(keep):
        hidden_grad += dot(down_in[:, k * edge : (k + 1) * edge], wd[0, k], ((1,), (1,)))
    hidden_grad = scale * hidden_grad
    sig = jax.nn.sigmoid(gate)
    act = gate * sig
    hidden = (act * up).astype(BF16)
    gate_signal = (hidden_grad * up * sig * (1.0 + gate * (1.0 - sig))).astype(BF16)
    up_signal = (hidden_grad * act).astype(BF16)

    def step(w, grad):
        grad = (scale * grad).astype(BF16).astype(F32)
        return (w.astype(F32) - LEARN_RATE * grad).astype(BF16)

    def side(i, w, signal, inputs, turned):
        grad = dot(signal, inputs, ((0,), (0,)))
        for k in range(keep):
            part = grad[:, k * edge : (k + 1) * edge]
            fresh[i, 0, k] = step(w[0, k], part.T if turned else part)

    side(2, wd, hidden, down_in, False)
    side(0, wg, gate_signal, gate_in, True)
    side(1, wu, up_signal, up_in, True)
    for w, signal, rows in ((wg, gate_signal, gate_rows), (wu, up_signal, up_rows)):
        for k in range(keep):
            back = dot(signal, w[0, k], ((1,), (1,)))
            columns = pl.ds(pl.multiple_of(rows[j, k] * edge, edge), edge)
            total[:, columns] += back


def chunk_step(offset, size, total, rows, x, g, weights):
    keep, edge = weights[0].shape[1:3]
    whole = pl.BlockSpec(x.shape, lambda j, *_: (0, 0))
    block = pl.BlockSpec((1, keep, edge, edge), lambda j, *_: (offset + j, 0, 0, 0))
    first = total is None
    return pl.pallas_call(
        functools.partial(step_kernel, offset, first, keep, edge),
        grid_spec=pltpu.PrefetchScalarGridSpec(
            num_scalar_prefetch=3,
            grid=(size,),
            in_specs=[whole, whole, block, block, block] + ([] if first else [whole]),
            out_specs=[pl.BlockSpec((3, 1, keep, edge, edge), lambda j, *_: (0, j, 0, 0, 0)), whole],
        ),
        out_shape=[
            jax.ShapeDtypeStruct((3, size, keep, edge, edge), BF16),
            jax.ShapeDtypeStruct(x.shape, F32),
        ],
        compiler_params=pltpu.CompilerParams(vmem_limit_bytes=VMEM_LIMIT),
        cost_estimate=pl.CostEstimate(flops=1, bytes_accessed=1, transcendentals=0),
    )(*rows, x, g, *weights, *([] if first else [total]))


def mean_kernel(own, peer, *rest):
    for i, out in enumerate(rest[-3:]):
        out[0] = ((own[i, 0].astype(F32) + peer[i, 0].astype(F32)) * 0.5).astype(BF16)


def chunk_mean(offset, own, peer, outs, shape):
    _, size, keep, edge, _ = own.shape
    part = pl.BlockSpec((3, 1, keep, edge, edge), lambda j: (0, j, 0, 0, 0))
    out = pl.BlockSpec((1, keep, edge, edge), lambda j: (offset + j, 0, 0, 0))
    given = [] if outs is None else list(outs)
    return pl.pallas_call(
        mean_kernel,
        grid=(size,),
        in_specs=[part, part] + [pl.BlockSpec(memory_space=pl.ANY)] * len(given),
        out_specs=[out] * 3,
        out_shape=[jax.ShapeDtypeStruct(shape, BF16)] * 3,
        input_output_aliases={2 + i: i for i in range(len(given))},
        compiler_params=pltpu.CompilerParams(vmem_limit_bytes=VMEM_LIMIT),
        cost_estimate=pl.CostEstimate(flops=1, bytes_accessed=1, transcendentals=0),
    )(own, peer, *given)


def sum_kernel(scale, own, *rest):
    out = rest[-1]
    value = scale * own[...]
    for part in rest[:-1]:
        value = value + part[...].astype(F32)
    out[...] = value.astype(BF16)


def summed_rows(scale, total):
    count = lax.axis_size("tp")
    me = lax.axis_index("tp")
    rows = total.shape[0] // count
    parts = []
    for turn in range(1, count):
        part = lax.dynamic_slice_in_dim(total, (me ^ turn) * rows, rows)
        pairs = [(source, source ^ turn) for source in range(count)]
        parts.append(lax.ppermute((scale * part).astype(BF16), "tp", pairs))
    own = lax.dynamic_slice_in_dim(total, me * rows, rows)
    return pl.pallas_call(
        functools.partial(sum_kernel, scale),
        out_shape=jax.ShapeDtypeStruct(own.shape, BF16),
        compiler_params=pltpu.CompilerParams(vmem_limit_bytes=VMEM_LIMIT),
        cost_estimate=pl.CostEstimate(flops=1, bytes_accessed=1, transcendentals=0),
    )(own, *parts)


def spans(count):
    first = min(FIRST, count)
    cuts = [first + (count - first) * i // LATER for i in range(LATER + 1)]
    return [(0, first)] + [(a, b - a) for a, b in zip(cuts, cuts[1:]) if b > a]


def exchanged(operands, distance):
    x, g, weights, rows = operands
    count = lax.axis_size("rep")
    pairs = [(source, (source + distance) % count) for source in range(count)]
    total = None
    own, peer = [], []
    for offset, size in spans(weights[0].shape[0]):
        fresh, total = chunk_step(offset, size, total, rows, x, g, weights)
        own.append(fresh)
        peer.append(lax.ppermute(fresh, "rep", pairs))
    keep, edge = weights[0].shape[1:3]
    input_grad = summed_rows((keep * edge) ** (-0.5), total)
    outs = None
    for (offset, _), mine, theirs in zip(spans(weights[0].shape[0]), own, peer):
        outs = chunk_mean(offset, mine, theirs, outs, weights[0].shape)
    return (input_grad, *outs)


def per_device(tokens, cotangent, gate_blocks, up_blocks, down_blocks, gate_rows, up_rows, down_columns, step_index):
    x, g = gathered_rows(tokens, cotangent)
    levels = lax.axis_size("rep").bit_length() - 1
    branches = [functools.partial(exchanged, distance=2**exponent) for exponent in range(levels)]
    operands = (x, g, (gate_blocks, up_blocks, down_blocks), (gate_rows, up_rows, down_columns))
    return tuple(lax.switch(step_index[0] % levels, branches, operands))


def solution(mesh):
    blocks = P(("rep", "tp"), None, None, None)
    table = P("tp", None)
    rows = P(("rep", "tp"), None)
    return jax.shard_map(
        per_device,
        mesh=mesh,
        in_specs=(rows, rows, blocks, blocks, blocks, table, table, table, P()),
        out_specs=(rows, blocks, blocks, blocks),
        check_vma=False,
    )
```

```python
import functools

import jax
import jax.numpy as jnp
from jax import lax
from jax.experimental import pallas as pl
from jax.experimental.pallas import tpu as pltpu
from jax.sharding import PartitionSpec as P

LEARN_RATE = 0.5
PIECES = 4
FIRST = 2
LATER = 4
VMEM_LIMIT = 60 * 1024 * 1024
F32 = jnp.float32
BF16 = jnp.bfloat16


def gather_kernel(rows, tok, cot, all_tok, all_cot, own_sem, sib_send, sib_recv, far_send, far_recv, fwd_send, fwd_recv):
    me = lax.axis_index("tp")
    sibling = me + 1 - 2 * lax.rem(me, 2)
    far = lax.rem(me + 2, 4)
    barrier = pltpu.get_barrier_semaphore()
    for other in (sibling, far):
        pl.semaphore_signal(barrier, inc=1, device_id={"tp": other}, device_id_type=pl.DeviceIdType.MESH)
    pl.semaphore_wait(barrier, 2)
    pairs = ((tok, all_tok), (cot, all_cot))
    part = rows // PIECES
    far_copies = []
    for a, (own, gathered) in enumerate(pairs):
        for i in range(PIECES):
            span = pl.ds(i * part, part)
            copy = pltpu.make_async_remote_copy(
                src_ref=own.at[span],
                dst_ref=gathered.at[me, span],
                send_sem=far_send.at[a, i],
                recv_sem=far_recv.at[a, i],
                device_id={"tp": far},
                device_id_type=pl.DeviceIdType.MESH,
            )
            copy.start()
            far_copies.append(copy)
    near_copies = []
    own_copies = []
    for a, (own, gathered) in enumerate(pairs):
        copy = pltpu.make_async_remote_copy(
            src_ref=own,
            dst_ref=gathered.at[me],
            send_sem=sib_send.at[a],
            recv_sem=sib_recv.at[a],
            device_id={"tp": sibling},
            device_id_type=pl.DeviceIdType.MESH,
        )
        copy.start()
        near_copies.append(copy)
        mine = pltpu.make_async_copy(own, gathered.at[me], own_sem.at[a])
        mine.start()
        own_copies.append(mine)
    forwards = []
    for a, (own, gathered) in enumerate(pairs):
        for i in range(PIECES):
            far_copies[a * PIECES + i].wait_recv()
            span = pl.ds(i * part, part)
            copy = pltpu.make_async_remote_copy(
                src_ref=gathered.at[far, span],
                dst_ref=gathered.at[far, span],
                send_sem=fwd_send.at[a, i],
                recv_sem=fwd_recv.at[a, i],
                device_id={"tp": sibling},
                device_id_type=pl.DeviceIdType.MESH,
            )
            copy.start()
            forwards.append(copy)
    for copy in far_copies:
        copy.wait_send()
    for copy in near_copies + own_copies + forwards:
        copy.wait()


def gathered_rows(tokens, cotangent):
    rows, width = tokens.shape
    count = lax.axis_size("tp")
    assert count == 4
    shape = jax.ShapeDtypeStruct((count, rows, width), tokens.dtype)
    dma = pltpu.SemaphoreType.DMA
    both = pl.pallas_call(
        functools.partial(gather_kernel, rows),
        out_shape=(shape, shape),
        in_specs=[pl.BlockSpec(memory_space=pl.ANY)] * 2,
        out_specs=(pl.BlockSpec(memory_space=pl.ANY),) * 2,
        scratch_shapes=[
            dma((2,)),
            dma((2,)),
            dma((2,)),
            dma((2, PIECES)),
            dma((2, PIECES)),
            dma((2, PIECES)),
            dma((2, PIECES)),
        ],
        compiler_params=pltpu.CompilerParams(collective_id=0, has_side_effects=True),
    )(tokens, cotangent)
    return [part.reshape(count * rows, width) for part in both]


def dot(a, b, dims):
    return lax.dot_general(a, b, (dims, ((), ())), preferred_element_type=F32)


def step_kernel(offset, first, keep, edge, table, x, g, wg, wu, wd, *rest):
    fresh, total = rest[-2:]
    scale = (keep * edge) ** (-0.5)
    j = offset + pl.program_id(0)
    count = table.shape[0] // (3 * keep)
    gate_rows, up_rows, down_columns = ((i * count + j) * keep for i in range(3))

    @pl.when(pl.program_id(0) == 0)
    def _():
        total[...] = jnp.zeros_like(total) if first else rest[0][...]

    def picked(source, rows):
        return jnp.concatenate(
            [source[:, pl.ds(pl.multiple_of(table[rows + k] * edge, edge), edge)] for k in range(keep)], axis=1
        )

    def flat(w):
        return w[0].reshape(keep * edge, edge)

    gate_in = picked(x, gate_rows)
    up_in = picked(x, up_rows)
    down_in = picked(g, down_columns)
    gate = scale * dot(gate_in, flat(wg), ((1,), (0,)))
    up = scale * dot(up_in, flat(wu), ((1,), (0,)))
    hidden_grad = jnp.zeros_like(gate)
    for k in range(keep):
        hidden_grad += dot(down_in[:, k * edge : (k + 1) * edge], wd[0, k], ((1,), (1,)))
    hidden_grad = scale * hidden_grad
    sig = jax.nn.sigmoid(gate)
    act = gate * sig
    hidden = (act * up).astype(BF16)
    gate_signal = (hidden_grad * up * sig * (1.0 + gate * (1.0 - sig))).astype(BF16)
    up_signal = (hidden_grad * act).astype(BF16)

    def step(w, grad):
        grad = (scale * grad).astype(BF16).astype(F32)
        return (w.astype(F32) - LEARN_RATE * grad).astype(BF16)

    def side(i, w, signal, inputs, turned):
        grad = dot(signal, inputs, ((0,), (0,)))
        for k in range(keep):
            part = grad[:, k * edge : (k + 1) * edge]
            fresh[i, 0, k] = step(w[0, k], part.T if turned else part)

    side(2, wd, hidden, down_in, False)
    side(0, wg, gate_signal, gate_in, True)
    side(1, wu, up_signal, up_in, True)
    for w, signal, rows in ((wg, gate_signal, gate_rows), (wu, up_signal, up_rows)):
        for k in range(keep):
            back = dot(signal, w[0, k], ((1,), (1,)))
            columns = pl.ds(pl.multiple_of(table[rows + k] * edge, edge), edge)
            total[:, columns] += back


def chunk_step(offset, size, total, table, x, g, weights, arrived):
    keep, edge = weights[0].shape[1:3]
    whole = pl.BlockSpec(x.shape, lambda j, *_: (0, 0))
    block = pl.BlockSpec((1, keep, edge, edge), lambda j, *_: (offset + j, 0, 0, 0))
    first = total is None
    return pl.pallas_call(
        functools.partial(step_kernel, offset, first, keep, edge),
        grid_spec=pltpu.PrefetchScalarGridSpec(
            num_scalar_prefetch=1,
            grid=(size,),
            in_specs=[whole, whole, block, block, block] + ([] if first else [whole])
            + [pl.BlockSpec(memory_space=pl.ANY)] * len(arrived),
            out_specs=[pl.BlockSpec((3, 1, keep, edge, edge), lambda j, *_: (0, j, 0, 0, 0)), whole],
        ),
        out_shape=[
            jax.ShapeDtypeStruct((3, size, keep, edge, edge), BF16),
            jax.ShapeDtypeStruct(x.shape, F32),
        ],
        compiler_params=pltpu.CompilerParams(vmem_limit_bytes=VMEM_LIMIT),
        cost_estimate=pl.CostEstimate(flops=1, bytes_accessed=1, transcendentals=0),
    )(table, x, g, *weights, *([] if first else [total]), *arrived)


def mean_kernel(own, peer, *rest):
    for i, out in enumerate(rest[-3:]):
        out[0] = ((own[i, 0].astype(F32) + peer[i, 0].astype(F32)) * 0.5).astype(BF16)


def chunk_mean(offset, own, peer, outs, shape):
    _, size, keep, edge, _ = own.shape
    part = pl.BlockSpec((3, 1, keep, edge, edge), lambda j: (0, j, 0, 0, 0))
    out = pl.BlockSpec((1, keep, edge, edge), lambda j: (offset + j, 0, 0, 0))
    given = [] if outs is None else list(outs)
    return pl.pallas_call(
        mean_kernel,
        grid=(size,),
        in_specs=[part, part] + [pl.BlockSpec(memory_space=pl.ANY)] * len(given),
        out_specs=[out] * 3,
        out_shape=[jax.ShapeDtypeStruct(shape, BF16)] * 3,
        input_output_aliases={2 + i: i for i in range(len(given))},
        compiler_params=pltpu.CompilerParams(vmem_limit_bytes=VMEM_LIMIT),
        cost_estimate=pl.CostEstimate(flops=1, bytes_accessed=1, transcendentals=0),
    )(own, peer, *given)


def sum_kernel(scale, own, *rest):
    out = rest[-1]
    value = scale * own[...]
    for part in rest[:-1]:
        value = value + part[...].astype(F32)
    out[...] = value.astype(BF16)


def summed_rows(scale, total):
    count = lax.axis_size("tp")
    me = lax.axis_index("tp")
    rows = total.shape[0] // count
    parts = []
    for turn in range(1, count):
        part = lax.dynamic_slice_in_dim(total, (me ^ turn) * rows, rows)
        pairs = [(source, source ^ turn) for source in range(count)]
        parts.append(lax.ppermute((scale * part).astype(BF16), "tp", pairs))
    own = lax.dynamic_slice_in_dim(total, me * rows, rows)
    return pl.pallas_call(
        functools.partial(sum_kernel, scale),
        out_shape=jax.ShapeDtypeStruct(own.shape, BF16),
        compiler_params=pltpu.CompilerParams(vmem_limit_bytes=VMEM_LIMIT),
        cost_estimate=pl.CostEstimate(flops=1, bytes_accessed=1, transcendentals=0),
    )(own, *parts)


def spans(count):
    first = min(FIRST, count)
    cuts = [first + (count - first) * i // LATER for i in range(LATER + 1)]
    return [(0, first)] + [(a, b - a) for a, b in zip(cuts, cuts[1:]) if b > a]


def exchanged(operands, distance):
    x, g, weights, table = operands
    count = lax.axis_size("rep")
    pairs = [(source, (source + distance) % count) for source in range(count)]
    total = None
    own, peer = [], []
    for offset, size in spans(weights[0].shape[0]):
        fresh, total = chunk_step(offset, size, total, table, x, g, weights, peer[-2:-1])
        own.append(fresh)
        peer.append(lax.ppermute(fresh, "rep", pairs))
    keep, edge = weights[0].shape[1:3]
    input_grad = summed_rows((keep * edge) ** (-0.5), total)
    outs = None
    for (offset, _), mine, theirs in zip(spans(weights[0].shape[0]), own, peer):
        outs = chunk_mean(offset, mine, theirs, outs, weights[0].shape)
    return (input_grad, *outs)


def per_device(tokens, cotangent, gate_blocks, up_blocks, down_blocks, gate_rows, up_rows, down_columns, step_index):
    table = jnp.concatenate([gate_rows, up_rows, down_columns]).reshape(-1)
    x, g = gathered_rows(tokens, cotangent)
    levels = lax.axis_size("rep").bit_length() - 1
    branches = [functools.partial(exchanged, distance=2**exponent) for exponent in range(levels)]
    operands = (x, g, (gate_blocks, up_blocks, down_blocks), table)
    return tuple(lax.switch(step_index[0] % levels, branches, operands))


def solution(mesh):
    blocks = P(("rep", "tp"), None, None, None)
    table = P("tp", None)
    rows = P(("rep", "tp"), None)
    return jax.shard_map(
        per_device,
        mesh=mesh,
        in_specs=(rows, rows, blocks, blocks, blocks, table, table, table, P()),
        out_specs=(rows, blocks, blocks, blocks),
        check_vma=False,
    )
```

```python
import functools

import jax
import jax.numpy as jnp
from jax import lax
from jax.experimental import pallas as pl
from jax.experimental.pallas import tpu as pltpu
from jax.sharding import PartitionSpec as P

LEARN_RATE = 0.5
PIECES = 4
FIRST = 2
LATER = 4
VMEM_LIMIT = 60 * 1024 * 1024
F32 = jnp.float32
BF16 = jnp.bfloat16


def gather_kernel(rows, tok, cot, all_tok, all_cot, own_sem, sib_send, sib_recv, far_send, far_recv, fwd_send, fwd_recv):
    me = lax.axis_index("tp")
    sibling = me + 1 - 2 * lax.rem(me, 2)
    far = lax.rem(me + 2, 4)
    barrier = pltpu.get_barrier_semaphore()
    for other in (sibling, far):
        pl.semaphore_signal(barrier, inc=1, device_id={"tp": other}, device_id_type=pl.DeviceIdType.MESH)
    pl.semaphore_wait(barrier, 2)
    pairs = ((tok, all_tok), (cot, all_cot))
    part = rows // PIECES
    far_copies = []
    for a, (own, gathered) in enumerate(pairs):
        for i in range(PIECES):
            span = pl.ds(i * part, part)
            copy = pltpu.make_async_remote_copy(
                src_ref=own.at[span],
                dst_ref=gathered.at[me, span],
                send_sem=far_send.at[a, i],
                recv_sem=far_recv.at[a, i],
                device_id={"tp": far},
                device_id_type=pl.DeviceIdType.MESH,
            )
            copy.start()
            far_copies.append(copy)
    near_copies = []
    own_copies = []
    for a, (own, gathered) in enumerate(pairs):
        copy = pltpu.make_async_remote_copy(
            src_ref=own,
            dst_ref=gathered.at[me],
            send_sem=sib_send.at[a],
            recv_sem=sib_recv.at[a],
            device_id={"tp": sibling},
            device_id_type=pl.DeviceIdType.MESH,
        )
        copy.start()
        near_copies.append(copy)
        mine = pltpu.make_async_copy(own, gathered.at[me], own_sem.at[a])
        mine.start()
        own_copies.append(mine)
    forwards = []
    for a, (own, gathered) in enumerate(pairs):
        for i in range(PIECES):
            far_copies[a * PIECES + i].wait_recv()
            span = pl.ds(i * part, part)
            copy = pltpu.make_async_remote_copy(
                src_ref=gathered.at[far, span],
                dst_ref=gathered.at[far, span],
                send_sem=fwd_send.at[a, i],
                recv_sem=fwd_recv.at[a, i],
                device_id={"tp": sibling},
                device_id_type=pl.DeviceIdType.MESH,
            )
            copy.start()
            forwards.append(copy)
    for copy in far_copies:
        copy.wait_send()
    for copy in near_copies + own_copies + forwards:
        copy.wait()


def gathered_rows(tokens, cotangent):
    rows, width = tokens.shape
    count = lax.axis_size("tp")
    assert count == 4
    shape = jax.ShapeDtypeStruct((count, rows, width), tokens.dtype)
    dma = pltpu.SemaphoreType.DMA
    both = pl.pallas_call(
        functools.partial(gather_kernel, rows),
        out_shape=(shape, shape),
        in_specs=[pl.BlockSpec(memory_space=pl.ANY)] * 2,
        out_specs=(pl.BlockSpec(memory_space=pl.ANY),) * 2,
        scratch_shapes=[
            dma((2,)),
            dma((2,)),
            dma((2,)),
            dma((2, PIECES)),
            dma((2, PIECES)),
            dma((2, PIECES)),
            dma((2, PIECES)),
        ],
        compiler_params=pltpu.CompilerParams(collective_id=0, has_side_effects=True),
    )(tokens, cotangent)
    return [part.reshape(count * rows, width) for part in both]


def dot(a, b, dims):
    return lax.dot_general(a, b, (dims, ((), ())), preferred_element_type=F32)


def step_kernel(offset, first, sums, keep, edge, table, x, g, wg, wu, wd, *rest):
    fresh, total = rest[-2:] if sums else (rest[-1], None)
    scale = (keep * edge) ** (-0.5)
    j = offset + pl.program_id(0)
    count = table.shape[0] // (3 * keep)
    gate_rows, up_rows, down_columns = ((i * count + j) * keep for i in range(3))

    if sums:

        @pl.when(pl.program_id(0) == 0)
        def _():
            total[...] = jnp.zeros_like(total) if first else rest[0][...]

    def picked(source, rows):
        return jnp.concatenate(
            [source[:, pl.ds(pl.multiple_of(table[rows + k] * edge, edge), edge)] for k in range(keep)], axis=1
        )

    def flat(w):
        return w[0].reshape(keep * edge, edge)

    gate_in = picked(x, gate_rows)
    up_in = picked(x, up_rows)
    down_in = picked(g, down_columns)
    gate = scale * dot(gate_in, flat(wg), ((1,), (0,)))
    up = scale * dot(up_in, flat(wu), ((1,), (0,)))
    hidden_grad = jnp.zeros_like(gate)
    for k in range(keep):
        hidden_grad += dot(down_in[:, k * edge : (k + 1) * edge], wd[0, k], ((1,), (1,)))
    hidden_grad = scale * hidden_grad
    sig = jax.nn.sigmoid(gate)
    act = gate * sig
    hidden = (act * up).astype(BF16)
    gate_signal = (hidden_grad * up * sig * (1.0 + gate * (1.0 - sig))).astype(BF16)
    up_signal = (hidden_grad * act).astype(BF16)

    def step(w, grad):
        grad = (scale * grad).astype(BF16).astype(F32)
        return (w.astype(F32) - LEARN_RATE * grad).astype(BF16)

    def side(i, w, signal, inputs, turned):
        grad = dot(signal, inputs, ((0,), (0,)))
        for k in range(keep):
            part = grad[:, k * edge : (k + 1) * edge]
            fresh[i, 0, k] = step(w[0, k], part.T if turned else part)

    side(2, wd, hidden, down_in, False)
    side(0, wg, gate_signal, gate_in, True)
    side(1, wu, up_signal, up_in, True)
    for w, signal, rows in ((wg, gate_signal, gate_rows), (wu, up_signal, up_rows)) if sums else ():
        for k in range(keep):
            back = dot(signal, w[0, k], ((1,), (1,)))
            columns = pl.ds(pl.multiple_of(table[rows + k] * edge, edge), edge)
            total[:, columns] += back


def chunk_step(offset, size, total, table, x, g, weights, arrived, sums=True):
    keep, edge = weights[0].shape[1:3]
    whole = pl.BlockSpec(x.shape, lambda j, *_: (0, 0))
    block = pl.BlockSpec((1, keep, edge, edge), lambda j, *_: (offset + j, 0, 0, 0))
    first = total is None
    return pl.pallas_call(
        functools.partial(step_kernel, offset, first, sums, keep, edge),
        grid_spec=pltpu.PrefetchScalarGridSpec(
            num_scalar_prefetch=1,
            grid=(size,),
            in_specs=[whole, whole, block, block, block] + ([] if first else [whole])
            + [pl.BlockSpec(memory_space=pl.ANY)] * len(arrived),
            out_specs=[pl.BlockSpec((3, 1, keep, edge, edge), lambda j, *_: (0, j, 0, 0, 0)), whole][: 1 + sums],
        ),
        out_shape=[
            jax.ShapeDtypeStruct((3, size, keep, edge, edge), BF16),
            jax.ShapeDtypeStruct(x.shape, F32),
        ][: 1 + sums],
        compiler_params=pltpu.CompilerParams(vmem_limit_bytes=VMEM_LIMIT),
        cost_estimate=pl.CostEstimate(flops=1, bytes_accessed=1, transcendentals=0),
    )(table, x, g, *weights, *([] if first else [total]), *arrived)


def mean_kernel(own, peer, *rest):
    for i, out in enumerate(rest[-3:]):
        out[0] = ((own[i, 0].astype(F32) + peer[i, 0].astype(F32)) * 0.5).astype(BF16)


def chunk_mean(offset, own, peer, outs, shape):
    _, size, keep, edge, _ = own.shape
    part = pl.BlockSpec((3, 1, keep, edge, edge), lambda j: (0, j, 0, 0, 0))
    out = pl.BlockSpec((1, keep, edge, edge), lambda j: (offset + j, 0, 0, 0))
    given = [] if outs is None else list(outs)
    return pl.pallas_call(
        mean_kernel,
        grid=(size,),
        in_specs=[part, part] + [pl.BlockSpec(memory_space=pl.ANY)] * len(given),
        out_specs=[out] * 3,
        out_shape=[jax.ShapeDtypeStruct(shape, BF16)] * 3,
        input_output_aliases={2 + i: i for i in range(len(given))},
        compiler_params=pltpu.CompilerParams(vmem_limit_bytes=VMEM_LIMIT),
        cost_estimate=pl.CostEstimate(flops=1, bytes_accessed=1, transcendentals=0),
    )(own, peer, *given)


def sum_kernel(scale, own, *rest):
    out = rest[-1]
    value = scale * own[...]
    for part in rest[:-1]:
        value = value + part[...].astype(F32)
    out[...] = value.astype(BF16)


def summed_rows(scale, total):
    count = lax.axis_size("tp")
    me = lax.axis_index("tp")
    rows = total.shape[0] // count
    parts = []
    for turn in range(1, count):
        part = lax.dynamic_slice_in_dim(total, (me ^ turn) * rows, rows)
        pairs = [(source, source ^ turn) for source in range(count)]
        parts.append(lax.ppermute((scale * part).astype(BF16), "tp", pairs))
    own = lax.dynamic_slice_in_dim(total, me * rows, rows)
    return pl.pallas_call(
        functools.partial(sum_kernel, scale),
        out_shape=jax.ShapeDtypeStruct(own.shape, BF16),
        compiler_params=pltpu.CompilerParams(vmem_limit_bytes=VMEM_LIMIT),
        cost_estimate=pl.CostEstimate(flops=1, bytes_accessed=1, transcendentals=0),
    )(own, *parts)


def spans(count):
    first = min(FIRST, count)
    cuts = [first + (count - first) * i // LATER for i in range(LATER + 1)]
    return [(0, first)] + [(a, b - a) for a, b in zip(cuts, cuts[1:]) if b > a]


def exchanged(operands, distance):
    x, g, weights, table = operands
    count = lax.axis_size("rep")
    pairs = [(source, (source + distance) % count) for source in range(count)]
    total = None
    own, peer = [], []
    for i, (offset, size) in enumerate(spans(weights[0].shape[0])):
        if i == 0:
            (fresh,) = chunk_step(offset, size, None, table, x, g, weights, [], sums=False)
        else:
            fresh, total = chunk_step(offset, size, total, table, x, g, weights, peer[-2:-1])
        own.append(fresh)
        peer.append(lax.ppermute(fresh, "rep", pairs))
        if i == 1:
            _, total = chunk_step(0, spans(weights[0].shape[0])[0][1], total, table, x, g, weights, [])
    keep, edge = weights[0].shape[1:3]
    input_grad = summed_rows((keep * edge) ** (-0.5), total)
    outs = None
    for (offset, _), mine, theirs in zip(spans(weights[0].shape[0]), own, peer):
        outs = chunk_mean(offset, mine, theirs, outs, weights[0].shape)
    return (input_grad, *outs)


def per_device(tokens, cotangent, gate_blocks, up_blocks, down_blocks, gate_rows, up_rows, down_columns, step_index):
    table = jnp.concatenate([gate_rows, up_rows, down_columns]).reshape(-1)
    x, g = gathered_rows(tokens, cotangent)
    levels = lax.axis_size("rep").bit_length() - 1
    branches = [functools.partial(exchanged, distance=2**exponent) for exponent in range(levels)]
    operands = (x, g, (gate_blocks, up_blocks, down_blocks), table)
    return tuple(lax.switch(step_index[0] % levels, branches, operands))


def solution(mesh):
    blocks = P(("rep", "tp"), None, None, None)
    table = P("tp", None)
    rows = P(("rep", "tp"), None)
    return jax.shard_map(
        per_device,
        mesh=mesh,
        in_specs=(rows, rows, blocks, blocks, blocks, table, table, table, P()),
        out_specs=(rows, blocks, blocks, blocks),
        check_vma=False,
    )
```
